128 devices in a mesh: chan: 16 (over y, z_lo, core), tm: 8 (over x, z_hi).
Axes of the slice: x: 4, y: 4, z: 4 (z_hi: 2, z_lo: 2; z = z_hi * 2 + z_lo), core: 2. Of those that a mesh axis runs over, the one named last changes fastest.
Arguments:
- record: bfloat16 [256, 1024, 1024], P('chan', 'tm'), may hold values from -500 to 500
- flags: int32 [256], P('chan'), may hold values 0 or 1
Outputs:
- correlation: float32 [256, 256, 512], P('chan', 'tm')
The draws below stay inside these ranges and needn't reach their ends.
Inputs may be any that keep to these rules, and one draw needn't show every extreme that they name: `flags`: 1 marks a usable channel, 0 a dead one.
All inputs are finite; a program needn't handle non-finite values. No bound on the sum of `flags` on one device may be relied on, other than what follows from the above.
Results may differ from the reference program's by a relative error of at most 0.0065.
Values may be sent and summed in bfloat16 or wider, within the bound.
No kernel may reach another device: no remote copies, remote signals or barrier semaphores. Data moves between devices by JAX's collectives and lax.ppermute only.
A program may use at most 256 MiB of HBM per device.

```python
import math
import jax
import jax.numpy as jnp
from jax import lax

WIN_DEV = 128
L = 1024
F = 256
LAGS = 512
HALF = 64
CHANNELS = 256
WINDOW_COUNT = 1024
N_TM = 8


def draw_record(key, part):
    key = jax.random.fold_in(key, 7)
    keys = jax.random.split(key, 6)
    shape = (CHANNELS, WINDOW_COUNT, L)
    base = jax.random.normal(keys[0], shape, jnp.float32)
    source = jax.random.normal(keys[1], (WINDOW_COUNT, L), jnp.float32)
    top = 10.0
    coupling = 0.7
    tilt = jax.random.uniform(keys[2], (CHANNELS, 1, 1), jnp.float32, -0.8, 0.8)
    colored = base + tilt * jnp.roll(base, 1, axis=2)
    delays = jax.random.randint(keys[3], (CHANNELS,), 0, L // 4)
    places = jnp.arange(L, dtype=jnp.int32)
    index = jnp.mod(places[None, :] - delays[:, None], L)
    moved = jnp.transpose(jnp.take(source, index, axis=1), (1, 0, 2))
    rows = jnp.exp(jax.random.uniform(keys[4], (CHANNELS, WINDOW_COUNT, 1), jnp.float32) * math.log(top))
    envelope = jnp.exp(jax.random.uniform(keys[5], shape, jnp.float32) * math.log(10.0))
    return jnp.clip(rows * envelope * (colored + coupling * moved), -500.0, 500.0).astype(jnp.bfloat16)


def touch_ends(array, own_key, low, high):
    index_at = [jax.random.randint(jax.random.fold_in(own_key, axis), (), 0, length) for axis, length in enumerate(array.shape)]
    widest = array.shape.index(max(array.shape))
    neighbour = index_at[:widest] + [(index_at[widest] + 1) % array.shape[widest]] + index_at[widest + 1:]
    return array.at[tuple(index_at)].set(low).at[tuple(neighbour)].set(high)


def setup_inputs(seed: int = 0) -> dict:
    seeds = jax.random.split(jax.random.key(seed), 3)
    return {
        "record": draw_record(jax.random.fold_in(seeds[2], 71), 0),
        "flags": touch_ends((jax.random.randint(seeds[1], (CHANNELS,), 0, 8) < 7).astype(jnp.int32), jax.random.fold_in(seeds[1], 1), 0, 1),
    }


def fourier_matrix(record_length):
    places = jnp.arange(record_length, dtype=jnp.int32)
    bins = jnp.arange(F, dtype=jnp.int32)
    phase = jnp.mod(places[:, None] * bins[None, :], record_length).astype(jnp.float32)
    angle = 2.0 * math.pi / record_length * phase
    return jnp.stack([jnp.cos(angle), -jnp.sin(angle)], axis=1).astype(jnp.bfloat16)

def lag_table(record_length, total_windows):
    bins = jnp.arange(F, dtype=jnp.int32)
    shifts = jnp.arange(LAGS, dtype=jnp.int32) - LAGS // 2
    phase = jnp.mod(bins[:, None] * shifts[None, :], record_length).astype(jnp.float32)
    angle = 2.0 * math.pi / record_length * phase
    factor = 1.0 / (F * total_windows)
    return jnp.stack([jnp.cos(angle) * factor, -jnp.sin(angle) * factor]).astype(jnp.bfloat16)

def whiten(record, flags):
    magnitude = jnp.abs(record).astype(jnp.float32)
    sums = lax.reduce_window(magnitude, jnp.float32(0.0), lax.add, (1, 1, 2 * HALF + 1), (1, 1, 1), [(0, 0), (0, 0), (HALF, HALF)])
    ones = jnp.ones((1, 1, L), jnp.float32)
    counts = lax.reduce_window(ones, jnp.float32(0.0), lax.add, (1, 1, 2 * HALF + 1), (1, 1, 1), [(0, 0), (0, 0), (HALF, HALF)])
    amplitude = sums / counts + 1e-05
    normalized = (record.astype(jnp.float32) / amplitude).astype(jnp.bfloat16)
    table = fourier_matrix(L).reshape(L, 2 * F)
    flat = jnp.dot(normalized.reshape(CHANNELS * WINDOW_COUNT, L), table, preferred_element_type=jnp.float32)
    spectrum = jnp.transpose(flat.reshape(CHANNELS, WINDOW_COUNT, 2, F), (2, 3, 0, 1))
    power = spectrum[0] * spectrum[0] + spectrum[1] * spectrum[1]
    padded = jnp.pad(power, ((2, 2), (0, 0), (0, 0)))
    smoothing = (padded[0:-4] + padded[1:-3] + padded[2:-2] + padded[3:-1] + padded[4:]) / 5.0
    level = lax.optimization_barrier(jnp.mean(power, axis=0, keepdims=True))
    scale = flags.astype(jnp.float32)[None, :, None] / jnp.sqrt(smoothing + 0.1 * level + 1e-06)
    return (spectrum * scale[None]).astype(jnp.bfloat16)

def cross_pair(local, remote):
    local_wide = local.astype(jnp.float32)
    remote_wide = remote.astype(jnp.float32)
    remote_swap = jnp.stack([-remote_wide[1], remote_wide[0]])
    real_part = jnp.einsum('sfcw,sfdw->fcd', local_wide, remote_wide)
    imag_part = jnp.einsum('sfcw,sfdw->fcd', local_wide, remote_swap)
    return jnp.stack([real_part, imag_part]).astype(jnp.bfloat16)

def reference(record, flags):
    white = whiten(record, flags)

    def add_block(block, total):
        start = (block * WIN_DEV).astype(jnp.int32)
        piece = lax.dynamic_slice_in_dim(white, start, WIN_DEV, 3)
        return total + cross_pair(piece, piece).astype(jnp.float32)
    total = jnp.zeros((2, F, CHANNELS, CHANNELS), jnp.float32)
    total = lax.fori_loop(0, N_TM, add_block, total)
    table = lag_table(L, WINDOW_COUNT).astype(jnp.float32)
    return jnp.einsum('sfcd,sft->cdt', total, table, precision=lax.Precision.HIGHEST)
```

```python
import math

import jax
import jax.numpy as jnp
import ml_dtypes
import numpy as np
from jax import lax
from jax.experimental import pallas as pl
from jax.experimental.pallas import tpu as pltpu
from jax.sharding import PartitionSpec as P

L = 1024
F = 256
LAGS = 512
HALF = 64
CHANNELS = 256
WINDOWS = 1024
BOTH = ("chan", "tm")

CB = 4
NC = 16
NW = 128
ND = 32
N_CHAN = 16
N_TM = 8
N_DEV = 128
MIB = 1 << 20


def dft_rows():
    phase = np.outer(np.arange(F), np.arange(L)) % L
    angle = 2.0 * math.pi / L * phase
    parts = np.stack([np.cos(angle), -np.sin(angle)])
    parts = parts.reshape(2, 8, 32, L).transpose(0, 2, 1, 3)
    return parts.reshape(2 * F, L).astype(ml_dtypes.bfloat16)


def lag_rows():
    shifts = np.arange(LAGS) - LAGS // 2
    angle = 2.0 * math.pi / L * (np.outer(np.arange(F), shifts) % L)
    factor = 1.0 / (F * WINDOWS)
    parts = np.stack([np.cos(angle) * factor, -np.sin(angle) * factor])
    parts = parts.reshape(2, 128, 2, LAGS).transpose(2, 0, 1, 3)
    return parts.reshape(2 * F, LAGS).astype(ml_dtypes.bfloat16)


def band_block():
    rows = np.arange(512)[:, None] - 128
    return (np.abs(rows - np.arange(256)[None, :]) <= HALF).astype(ml_dtypes.bfloat16)


def inverse_counts():
    places = np.arange(L)
    counts = np.minimum(places + HALF, L - 1) - np.maximum(places - HALF, 0) + 1
    return (1.0 / counts).astype(np.float32).reshape(1, L)


def whiten_kernel(flags_ref, record_ref, band_ref, inverse_ref, table_ref, out_ref, wide):
    step = pl.program_id(0)
    rows = CB * NW
    x = record_ref[...].reshape(rows, L)
    magnitude = jnp.abs(x)
    pieces = []
    for j in range(4):
        low, high = max(256 * j - 128, 0), min(256 * j + 384, L)
        first = low - (256 * j - 128)
        sums = jnp.dot(
            magnitude[:, low:high],
            band_ref[first : first + high - low, :],
            preferred_element_type=jnp.float32,
        )
        cut = slice(256 * j, 256 * j + 256)
        amplitude = sums * inverse_ref[:, cut] + 1e-05
        pieces.append((x[:, cut].astype(jnp.float32) / amplitude).astype(jnp.bfloat16))
    normed = jnp.concatenate(pieces, axis=1)
    spectrum = lax.dot_general(
        table_ref[...], normed, (((1,), (1,)), ((), ())), preferred_element_type=jnp.float32
    )
    lanes = lax.broadcasted_iota(jnp.int32, (8, NW), 0)
    for c in range(CB):
        cut = slice(c * NW, (c + 1) * NW)
        real = [spectrum[8 * v : 8 * v + 8, cut] for v in range(32)]
        imag = [spectrum[F + 8 * v : F + 8 * v + 8, cut] for v in range(32)]
        power = [r * r + i * i for r, i in zip(real, imag)]
        before = [jnp.where(lanes == 0, 0.0, pltpu.roll(power[v], 1, 0)) for v in (30, 31)]
        after = [jnp.where(lanes == 7, 0.0, pltpu.roll(power[v], 7, 0)) for v in (0, 1)]
        padded = before + power + after
        total = power[0]
        for v in range(1, 32):
            total = total + power[v]
        floor = jnp.sum(total, axis=0, keepdims=True) * (0.1 / F) + 1e-06
        channel = step * CB + c
        flag = flags_ref[channel].astype(jnp.float32)
        for v in range(32):
            smooth = padded[v] + padded[v + 1] + padded[v + 2] + padded[v + 3] + padded[v + 4]
            scale = lax.rsqrt(smooth * 0.2 + floor) * flag
            for s, part in ((0, real), (1, imag)):
                place = ((v // 2) * 4 + s * 2 + v % 2) * NC + channel
                wide[pl.ds(place, 8, stride=64 * NC), :] = part[v] * scale

    @pl.when(step == pl.num_programs(0) - 1)
    def _():
        out_ref[...] = wide[...].astype(jnp.bfloat16)


def whiten(record, flags):
    rows = 2 * F * NC
    white = pl.pallas_call(
        whiten_kernel,
        grid=(NC // CB,),
        in_specs=[
            pl.BlockSpec(memory_space=pltpu.SMEM),
            pl.BlockSpec((CB, NW, L), lambda i: (i, 0, 0)),
            pl.BlockSpec((512, 256), lambda i: (0, 0)),
            pl.BlockSpec((1, L), lambda i: (0, 0)),
            pl.BlockSpec((2 * F, L), lambda i: (0, 0)),
        ],
        out_specs=pl.BlockSpec((rows, NW), lambda i: (0, 0)),
        out_shape=jax.ShapeDtypeStruct((rows, NW), jnp.bfloat16),
        scratch_shapes=[pltpu.VMEM((rows, NW), jnp.float32)],
        compiler_params=pltpu.CompilerParams(vmem_limit_bytes=40 * MIB),
        cost_estimate=pl.CostEstimate(flops=2 * 2048 * 1024 * 1024, bytes_accessed=8 * MIB, transcendentals=1 << 21),
    )(flags, record, band_block(), inverse_counts(), dft_rows())
    return white.reshape(N_DEV, 4, NC, NW)


def cross_kernel(white_ref, out_ref):
    spectra = []
    for g in range(2):
        parts = []
        for s in range(2):
            for j in range(N_TM):
                parts.append(white_ref[:, j, 2 * s + g].reshape(CHANNELS, NW))
        local = jnp.concatenate(parts, axis=1)
        turned = jnp.concatenate([-p for p in parts[N_TM:]] + parts[:N_TM], axis=1)
        remote = []
        for j in range(N_TM):
            cut = slice(ND * j, ND * j + ND)
            remote += [local[cut], turned[cut]]
        spectra.append(
            lax.dot_general(
                local, jnp.concatenate(remote, axis=0), (((1,), (1,)), ((), ())), preferred_element_type=jnp.float32
            )
        )
    for j in range(N_TM):
        cut = slice(2 * ND * j, 2 * ND * (j + 1))
        block = jnp.concatenate([spectra[0][:, cut], spectra[1][:, cut]], axis=1)
        out_ref[:, j] = block.astype(jnp.bfloat16).reshape(N_CHAN, NC, 4 * ND)


def cross(white):
    out = pl.pallas_call(
        cross_kernel,
        out_shape=jax.ShapeDtypeStruct((N_CHAN, N_TM, NC, 4 * ND), jnp.bfloat16),
        compiler_params=pltpu.CompilerParams(vmem_limit_bytes=40 * MIB),
        cost_estimate=pl.CostEstimate(flops=1 << 30, bytes_accessed=3 * MIB, transcendentals=0),
    )(white.reshape(N_CHAN, N_TM, 4, NC, NW))
    return out.reshape(N_DEV, NC, 4 * ND)


def lags_kernel(cross_ref, table_ref, out_ref, wide):
    wide[...] = cross_ref[...].astype(jnp.float32).reshape(N_DEV * NC, 4 * ND)
    rows = []
    for c in range(NC):
        bins = wide[pl.ds(c, N_DEV, stride=NC), :].T.astype(jnp.bfloat16)
        rows.append(jnp.concatenate([bins[ND * q : ND * q + ND] for q in range(4)], axis=1))
    out = jnp.dot(jnp.concatenate(rows, axis=0), table_ref[...], preferred_element_type=jnp.float32)
    out_ref[...] = out.reshape(NC, ND, LAGS)


def to_lags(spectra):
    return pl.pallas_call(
        lags_kernel,
        out_shape=jax.ShapeDtypeStruct((NC, ND, LAGS), jnp.float32),
        scratch_shapes=[pltpu.VMEM((N_DEV * NC, 4 * ND), jnp.float32)],
        compiler_params=pltpu.CompilerParams(vmem_limit_bytes=40 * MIB),
        cost_estimate=pl.CostEstimate(flops=1 << 28, bytes_accessed=2 * MIB, transcendentals=0),
    )(spectra, lag_rows())


def per_device(record, flags):
    white = lax.all_to_all(whiten(record, flags), BOTH, 0, 0, tiled=True)
    spectra = lax.all_to_all(cross(white), BOTH, 0, 0, tiled=True)
    return to_lags(spectra)


def solution(mesh):
    return jax.shard_map(
        per_device,
        mesh=mesh,
        in_specs=(P("chan", "tm", None), P("chan")),
        out_specs=P("chan", "tm", None),
        check_vma=False,
    )
```

```python
import math

import jax
import jax.numpy as jnp
import ml_dtypes
import numpy as np
from jax import lax
from jax.experimental import pallas as pl
from jax.experimental.pallas import tpu as pltpu
from jax.sharding import PartitionSpec as P

L = 1024
F = 256
LAGS = 512
HALF = 64
CHANNELS = 256
WINDOWS = 1024
BOTH = ("chan", "tm")

SUB = 2
PITCH = 17
NC = 16
NW = 128
ND = 32
N_CHAN = 16
N_TM = 8
N_DEV = 128
MIB = 1 << 20


def dft_rows():
    phase = np.outer(np.arange(F), np.arange(L // 2)) % L
    angle = 2.0 * math.pi / L * phase
    parts = np.stack([np.cos(angle), -np.sin(angle)])
    parts = parts.reshape(2, 8, 16, 2, L // 2).transpose(3, 0, 2, 1, 4)
    return parts.reshape(2, F, L // 2).astype(ml_dtypes.bfloat16)


def lag_rows():
    shifts = np.arange(LAGS) - LAGS // 2
    angle = 2.0 * math.pi / L * (np.outer(np.arange(F), shifts) % L)
    factor = 1.0 / (F * WINDOWS)
    parts = np.stack([np.cos(angle) * factor, -np.sin(angle) * factor])
    parts = parts.reshape(2, 128, 2, LAGS).transpose(2, 0, 1, 3)
    return parts.reshape(2 * F, LAGS).astype(ml_dtypes.bfloat16)


def band_block():
    rows = np.arange(512)[:, None] - 128
    return (np.abs(rows - np.arange(256)[None, :]) <= HALF).astype(ml_dtypes.bfloat16)


def normalise(record, band):
    x = record.reshape(SUB * NW, L)
    magnitude = jnp.abs(x)
    quarters = []
    for j in range(4):
        low, high = max(256 * j - 128, 0), min(256 * j + 384, L)
        first = low - (256 * j - 128)
        sums = jnp.dot(
            magnitude[:, low:high],
            band[first : first + high - low, :],
            preferred_element_type=jnp.float32,
        )
        places = 256 * j + lax.broadcasted_iota(jnp.int32, (1, 256), 1)
        counts = jnp.minimum(places + HALF, L - 1) - jnp.maximum(places - HALF, 0) + 1
        amplitude = sums * (1.0 / counts.astype(jnp.float32)) + 1e-05
        quarters.append(x[:, 256 * j : 256 * j + 256].astype(jnp.float32) / amplitude)
    even = [(quarters[q] + quarters[q + 2]).astype(jnp.bfloat16) for q in range(2)]
    odd = [(quarters[q] - quarters[q + 2]).astype(jnp.bfloat16) for q in range(2)]
    return jnp.concatenate(even, axis=1), jnp.concatenate(odd, axis=1)


def transform(table, halves):
    return [
        lax.dot_general(table[p], halves[p], (((1,), (1,)), ((), ())), preferred_element_type=jnp.float32)
        for p in range(2)
    ]


def store_white(wide, spectra, flag, channel):
    lanes = lax.broadcasted_iota(jnp.int32, (8, NW), 0)
    place = [8 * (v // 2) for v in range(32)]
    real = [spectra[v % 2][place[v] : place[v] + 8] for v in range(32)]
    imag = [spectra[v % 2][F // 2 + place[v] : F // 2 + place[v] + 8] for v in range(32)]
    power = [r * r + i * i for r, i in zip(real, imag)]
    before = [jnp.where(lanes == 0, 0.0, pltpu.roll(power[v], 1, 0)) for v in (30, 31)]
    after = [jnp.where(lanes == 7, 0.0, pltpu.roll(power[v], 7, 0)) for v in (0, 1)]
    padded = before + power + after
    total = power[0]
    for v in range(1, 32):
        total = total + power[v]
    floor = jnp.sum(total, axis=0, keepdims=True) * (0.1 / F) + 1e-06
    for v in range(32):
        smooth = padded[v] + padded[v + 1] + padded[v + 2] + padded[v + 3] + padded[v + 4]
        scale = lax.rsqrt(smooth * 0.2 + floor) * flag
        for s, part in ((0, real), (1, imag)):
            wide[pl.ds((2 * v + s) * 8 * PITCH + channel, 8, stride=PITCH), :] = part[v] * scale


def whiten_kernel(flags_hbm, record_hbm, band_hbm, table_hbm, out_ref, record, band, table, wide, flags, sems):
    count = NC // SUB
    parts = [pl.ds(t * SUB, SUB) for t in range(count)]
    copies = [pltpu.make_async_copy(record_hbm.at[p], record.at[p], sems.at[t]) for t, p in enumerate(parts)]
    copies += [
        pltpu.make_async_copy(band_hbm, band, sems.at[count]),
        pltpu.make_async_copy(table_hbm, table, sems.at[count + 1]),
        pltpu.make_async_copy(flags_hbm, flags, sems.at[count + 2]),
    ]
    for t in [0, count, 1, count + 1, count + 2, *range(2, count)]:
        copies[t].start()
    copies[count].wait()
    halves, spectra = {}, {}
    for t in range(count + 2):
        if t < count:
            copies[t].wait()
            halves[t] = normalise(record[t * SUB : (t + 1) * SUB], band)
        if t == 1:
            copies[count + 1].wait()
        if t == 2:
            copies[count + 2].wait()
        if 0 <= t - 1 < count:
            spectra[t - 1] = transform(table, halves.pop(t - 1))
        if 0 <= t - 2 < count:
            even, odd = spectra.pop(t - 2)
            for c in range(SUB):
                cut = slice(c * NW, (c + 1) * NW)
                channel = (t - 2) * SUB + c
                store_white(wide, (even[:, cut], odd[:, cut]), flags[channel].astype(jnp.float32), channel)
    for f in range(F):
        for s in range(2):
            place = ((2 * (f % 32) + s) * 8 + f // 32) * PITCH
            row = ((f // 2) * 4 + 2 * s + f % 2) * NC
            out_ref[row : row + NC, :] = wide[place : place + NC, :].astype(jnp.bfloat16)


def whiten(record, flags):
    rows = 2 * F * NC
    white = pl.pallas_call(
        whiten_kernel,
        in_specs=[pl.BlockSpec(memory_space=pltpu.HBM)] * 4,
        out_specs=pl.BlockSpec(memory_space=pltpu.VMEM),
        out_shape=jax.ShapeDtypeStruct((rows, NW), jnp.bfloat16),
        scratch_shapes=[
            pltpu.VMEM((NC, NW, L), jnp.bfloat16),
            pltpu.VMEM((512, 256), jnp.bfloat16),
            pltpu.VMEM((2, F, L // 2), jnp.bfloat16),
            pltpu.VMEM((2 * F * PITCH, NW), jnp.float32),
            pltpu.SMEM((NC,), jnp.int32),
            pltpu.SemaphoreType.DMA((NC // SUB + 3,)),
        ],
        compiler_params=pltpu.CompilerParams(vmem_limit_bytes=40 * MIB),
        cost_estimate=pl.CostEstimate(flops=2 * 2048 * 1024 * 1024, bytes_accessed=8 * MIB, transcendentals=1 << 21),
    )(*[pltpu.with_memory_space_constraint(jnp.asarray(a), pltpu.HBM) for a in (flags, record, band_block(), dft_rows())])
    return white.reshape(N_DEV, 4, NC, NW)


def cross_kernel(white_ref, out_ref):
    spectra = []
    for g in range(2):
        parts = []
        for s in range(2):
            for j in range(N_TM):
                parts.append(white_ref[:, j, 2 * s + g].reshape(CHANNELS, NW))
        local = jnp.concatenate(parts, axis=1)
        turned = jnp.concatenate([-p for p in parts[N_TM:]] + parts[:N_TM], axis=1)
        remote = []
        for j in range(N_TM):
            cut = slice(ND * j, ND * j + ND)
            remote += [local[cut], turned[cut]]
        spectra.append(
            lax.dot_general(
                local, jnp.concatenate(remote, axis=0), (((1,), (1,)), ((), ())), preferred_element_type=jnp.float32
            )
        )
    for j in range(N_TM):
        cut = slice(2 * ND * j, 2 * ND * (j + 1))
        block = jnp.concatenate([spectra[0][:, cut], spectra[1][:, cut]], axis=1)
        out_ref[:, j] = block.astype(jnp.bfloat16).reshape(N_CHAN, NC, 4 * ND)


def cross(white):
    out = pl.pallas_call(
        cross_kernel,
        out_shape=jax.ShapeDtypeStruct((N_CHAN, N_TM, NC, 4 * ND), jnp.bfloat16),
        compiler_params=pltpu.CompilerParams(vmem_limit_bytes=40 * MIB),
        cost_estimate=pl.CostEstimate(flops=1 << 30, bytes_accessed=3 * MIB, transcendentals=0),
    )(white.reshape(N_CHAN, N_TM, 4, NC, NW))
    return out.reshape(N_DEV, NC, 4 * ND)


def lags_kernel(cross_ref, table_ref, out_ref, wide):
    wide[...] = cross_ref[...].astype(jnp.float32).reshape(N_DEV * NC, 4 * ND)
    rows = []
    for c in range(NC):
        bins = wide[pl.ds(c, N_DEV, stride=NC), :].T.astype(jnp.bfloat16)
        rows.append(jnp.concatenate([bins[ND * q : ND * q + ND] for q in range(4)], axis=1))
    out = jnp.dot(jnp.concatenate(rows, axis=0), table_ref[...], preferred_element_type=jnp.float32)
    out_ref[...] = out.reshape(NC, ND, LAGS)


def to_lags(spectra):
    return pl.pallas_call(
        lags_kernel,
        out_shape=jax.ShapeDtypeStruct((NC, ND, LAGS), jnp.float32),
        scratch_shapes=[pltpu.VMEM((N_DEV * NC, 4 * ND), jnp.float32)],
        compiler_params=pltpu.CompilerParams(vmem_limit_bytes=40 * MIB),
        cost_estimate=pl.CostEstimate(flops=1 << 28, bytes_accessed=2 * MIB, transcendentals=0),
    )(spectra, lag_rows())


def per_device(record, flags):
    white = lax.all_to_all(whiten(record, flags), BOTH, 0, 0, tiled=True)
    spectra = lax.all_to_all(cross(white), BOTH, 0, 0, tiled=True)
    return to_lags(spectra)


def solution(mesh):
    return jax.shard_map(
        per_device,
        mesh=mesh,
        in_specs=(P("chan", "tm", None), P("chan")),
        out_specs=P("chan", "tm", None),
        check_vma=False,
    )
```

```python
import math

import jax
import jax.numpy as jnp
import ml_dtypes
import numpy as np
from jax import lax
from jax.experimental import pallas as pl
from jax.experimental.pallas import tpu as pltpu
from jax.sharding import PartitionSpec as P

L = 1024
F = 256
LAGS = 512
HALF = 64
CHANNELS = 256
WINDOWS = 1024
BOTH = ("chan", "tm")

SUB = 2
PITCH = 17
NC = 16
NW = 128
ND = 32
N_CHAN = 16
N_TM = 8
N_DEV = 128
N_OUT = 4
MIB = 1 << 20


def dft_rows():
    phase = np.outer(np.arange(F), np.arange(L // 2)) % L
    angle = 2.0 * math.pi / L * phase
    parts = np.stack([np.cos(angle), -np.sin(angle)])
    parts = parts.reshape(2, 8, 16, 2, L // 2).transpose(3, 0, 2, 1, 4)
    return parts.reshape(2, F, L // 2).astype(ml_dtypes.bfloat16)


def lag_rows():
    shifts = np.arange(LAGS) - LAGS // 2
    angle = 2.0 * math.pi / L * (np.outer(np.arange(F), shifts) % L)
    factor = 1.0 / (F * WINDOWS)
    parts = np.stack([np.cos(angle) * factor, -np.sin(angle) * factor])
    parts = parts.reshape(2, 128, 2, LAGS).transpose(2, 0, 1, 3)
    return parts.reshape(2 * F, LAGS).astype(ml_dtypes.bfloat16)


def band_block():
    rows = np.arange(512)[:, None] - 128
    return (np.abs(rows - np.arange(256)[None, :]) <= HALF).astype(ml_dtypes.bfloat16)


def normalise(record, band):
    x = record.reshape(SUB * NW, L)
    magnitude = jnp.abs(x)
    quarters = []
    for j in range(4):
        low, high = max(256 * j - 128, 0), min(256 * j + 384, L)
        first = low - (256 * j - 128)
        sums = jnp.dot(
            magnitude[:, low:high],
            band[first : first + high - low, :],
            preferred_element_type=jnp.float32,
        )
        places = 256 * j + lax.broadcasted_iota(jnp.int32, (1, 256), 1)
        counts = jnp.minimum(places + HALF, L - 1) - jnp.maximum(places - HALF, 0) + 1
        amplitude = sums * (1.0 / counts.astype(jnp.float32)) + 1e-05
        quarters.append(x[:, 256 * j : 256 * j + 256].astype(jnp.float32) / amplitude)
    even = [(quarters[q] + quarters[q + 2]).astype(jnp.bfloat16) for q in range(2)]
    odd = [(quarters[q] - quarters[q + 2]).astype(jnp.bfloat16) for q in range(2)]
    return jnp.concatenate(even, axis=1), jnp.concatenate(odd, axis=1)


def transform(table, halves):
    return [
        lax.dot_general(table[p], halves[p], (((1,), (1,)), ((), ())), preferred_element_type=jnp.float32)
        for p in range(2)
    ]


def store_white(wide, spectra, flag, channel):
    lanes = lax.broadcasted_iota(jnp.int32, (8, NW), 0)
    place = [8 * (v // 2) for v in range(32)]
    real = [spectra[v % 2][place[v] : place[v] + 8] for v in range(32)]
    imag = [spectra[v % 2][F // 2 + place[v] : F // 2 + place[v] + 8] for v in range(32)]
    power = [r * r + i * i for r, i in zip(real, imag)]
    before = [jnp.where(lanes == 0, 0.0, pltpu.roll(power[v], 1, 0)) for v in (30, 31)]
    after = [jnp.where(lanes == 7, 0.0, pltpu.roll(power[v], 7, 0)) for v in (0, 1)]
    padded = before + power + after
    total = power[0]
    for v in range(1, 32):
        total = total + power[v]
    floor = jnp.sum(total, axis=0, keepdims=True) * (0.1 / F) + 1e-06
    for v in range(32):
        smooth = padded[v] + padded[v + 1] + padded[v + 2] + padded[v + 3] + padded[v + 4]
        scale = lax.rsqrt(smooth * 0.2 + floor) * flag
        for s, part in ((0, real), (1, imag)):
            wide[pl.ds((2 * v + s) * 8 * PITCH + channel, 8, stride=PITCH), :] = part[v] * scale


def whiten_kernel(flags_hbm, record_hbm, band_hbm, table_hbm, out_ref, record, band, table, wide, flags, sems):
    count = NC // SUB
    parts = [pl.ds(t * SUB, SUB) for t in range(count)]
    copies = [pltpu.make_async_copy(record_hbm.at[p], record.at[p], sems.at[t]) for t, p in enumerate(parts)]
    copies += [
        pltpu.make_async_copy(band_hbm, band, sems.at[count]),
        pltpu.make_async_copy(table_hbm, table, sems.at[count + 1]),
        pltpu.make_async_copy(flags_hbm, flags, sems.at[count + 2]),
    ]
    for t in [0, 1, count, count + 1, count + 2, *range(2, count)]:
        copies[t].start()
    halves, spectra = {}, {}
    for t in range(count + 2):
        if t < count:
            if t == 0:
                for copy in copies[:2] + copies[count : count + 2]:
                    copy.wait()
            if t == 2:
                for copy in copies[2:count] + copies[count + 2 :]:
                    copy.wait()
            halves[t] = normalise(record[t * SUB : (t + 1) * SUB], band)
        if 0 <= t - 1 < count:
            spectra[t - 1] = transform(table, halves.pop(t - 1))
        if 0 <= t - 2 < count:
            even, odd = spectra.pop(t - 2)
            for c in range(SUB):
                cut = slice(c * NW, (c + 1) * NW)
                channel = (t - 2) * SUB + c
                store_white(wide, (even[:, cut], odd[:, cut]), flags[channel].astype(jnp.float32), channel)
    for f in range(F):
        for s in range(2):
            place = ((2 * (f % 32) + s) * 8 + f // 32) * PITCH
            row = ((f // 2) * 4 + 2 * s + f % 2) * NC
            out_ref[row : row + NC, :] = wide[place : place + NC, :].astype(jnp.bfloat16)


def whiten(record, flags):
    rows = 2 * F * NC
    white = pl.pallas_call(
        whiten_kernel,
        in_specs=[pl.BlockSpec(memory_space=pltpu.HBM)] * 4,
        out_specs=pl.BlockSpec(memory_space=pltpu.VMEM),
        out_shape=jax.ShapeDtypeStruct((rows, NW), jnp.bfloat16),
        scratch_shapes=[
            pltpu.VMEM((NC, NW, L), jnp.bfloat16),
            pltpu.VMEM((512, 256), jnp.bfloat16),
            pltpu.VMEM((2, F, L // 2), jnp.bfloat16),
            pltpu.VMEM((2 * F * PITCH, NW), jnp.float32),
            pltpu.SMEM((NC,), jnp.int32),
            pltpu.SemaphoreType.DMA((NC // SUB + 3,)),
        ],
        compiler_params=pltpu.CompilerParams(vmem_limit_bytes=40 * MIB),
        cost_estimate=pl.CostEstimate(flops=2 * 2048 * 1024 * 1024, bytes_accessed=8 * MIB, transcendentals=1 << 21),
    )(*[pltpu.with_memory_space_constraint(jnp.asarray(a), pltpu.HBM) for a in (flags, record, band_block(), dft_rows())])
    return white.reshape(N_DEV, 4, NC, NW)


def cross_kernel(white_ref, out_ref):
    spectra = []
    for g in range(2):
        parts = []
        for s in range(2):
            for j in range(N_TM):
                parts.append(white_ref[:, j, 2 * s + g].reshape(CHANNELS, NW))
        local = jnp.concatenate(parts, axis=1)
        turned = jnp.concatenate([-p for p in parts[N_TM:]] + parts[:N_TM], axis=1)
        remote = []
        for j in range(N_TM):
            cut = slice(ND * j, ND * j + ND)
            remote += [local[cut], turned[cut]]
        spectra.append(
            lax.dot_general(
                local, jnp.concatenate(remote, axis=0), (((1,), (1,)), ((), ())), preferred_element_type=jnp.float32
            )
        )
    for j in range(N_TM):
        cut = slice(2 * ND * j, 2 * ND * (j + 1))
        block = jnp.concatenate([spectra[0][:, cut], spectra[1][:, cut]], axis=1)
        out_ref[:, j] = block.astype(jnp.bfloat16).reshape(N_CHAN, NC, 4 * ND)


def cross(white):
    out = pl.pallas_call(
        cross_kernel,
        out_shape=jax.ShapeDtypeStruct((N_CHAN, N_TM, NC, 4 * ND), jnp.bfloat16),
        compiler_params=pltpu.CompilerParams(vmem_limit_bytes=40 * MIB),
        cost_estimate=pl.CostEstimate(flops=1 << 30, bytes_accessed=3 * MIB, transcendentals=0),
    )(white.reshape(N_CHAN, N_TM, 4, NC, NW))
    return out.reshape(N_DEV, NC, 4 * ND)


def lags_kernel(cross_ref, table_ref, out_hbm, wide, lags, sems):
    for k in range(N_DEV):
        wide[k * PITCH : k * PITCH + NC, :] = cross_ref[k].astype(jnp.float32)
    copies = []
    for n in range(N_OUT):
        rows = []
        for c in range(n * NC // N_OUT, (n + 1) * NC // N_OUT):
            bins = wide[pl.ds(c, N_DEV, stride=PITCH), :].T.astype(jnp.bfloat16)
            rows.append(jnp.concatenate([bins[ND * q : ND * q + ND] for q in range(4)], axis=1))
        out = jnp.dot(jnp.concatenate(rows, axis=0), table_ref[...], preferred_element_type=jnp.float32)
        part = pl.ds(n * NC // N_OUT, NC // N_OUT)
        lags[part] = out.reshape(NC // N_OUT, ND, LAGS)
        copies.append(pltpu.make_async_copy(lags.at[part], out_hbm.at[part], sems.at[n]))
        copies[n].start()
    for copy in copies:
        copy.wait()


def to_lags(spectra):
    return pl.pallas_call(
        lags_kernel,
        out_shape=jax.ShapeDtypeStruct((NC, ND, LAGS), jnp.float32),
        out_specs=pl.BlockSpec(memory_space=pltpu.HBM),
        scratch_shapes=[
            pltpu.VMEM((N_DEV * PITCH, 4 * ND), jnp.float32),
            pltpu.VMEM((NC, ND, LAGS), jnp.float32),
            pltpu.SemaphoreType.DMA((N_OUT,)),
        ],
        compiler_params=pltpu.CompilerParams(vmem_limit_bytes=40 * MIB),
        cost_estimate=pl.CostEstimate(flops=1 << 28, bytes_accessed=2 * MIB, transcendentals=0),
    )(spectra, lag_rows())


def per_device(record, flags):
    white = lax.all_to_all(whiten(record, flags), BOTH, 0, 0, tiled=True)
    spectra = lax.all_to_all(cross(white), BOTH, 0, 0, tiled=True)
    return to_lags(spectra)


def solution(mesh):
    return jax.shard_map(
        per_device,
        mesh=mesh,
        in_specs=(P("chan", "tm", None), P("chan")),
        out_specs=P("chan", "tm", None),
        check_vma=False,
    )
```

```python
import math

import jax
import jax.numpy as jnp
import ml_dtypes
import numpy as np
from jax import lax
from jax.experimental import pallas as pl
from jax.experimental.pallas import tpu as pltpu
from jax.sharding import PartitionSpec as P

L = 1024
F = 256
LAGS = 512
HALF = 64
CHANNELS = 256
WINDOWS = 1024
BOTH = ("chan", "tm")

SUB = 2
PITCH = 17
NC = 16
NW = 128
ND = 32
N_CHAN = 16
N_TM = 8
N_DEV = 128
N_OUT = 4
MIB = 1 << 20


def dft_rows():
    phase = np.outer(np.arange(F), np.arange(L // 2)) % L
    angle = 2.0 * math.pi / L * phase
    parts = np.stack([np.cos(angle), -np.sin(angle)])
    parts = parts.reshape(2, 8, 16, 2, L // 2).transpose(3, 0, 2, 1, 4)
    return parts.reshape(2, F, L // 2).astype(ml_dtypes.bfloat16)


def lag_rows():
    shifts = np.arange(LAGS) - LAGS // 2
    angle = 2.0 * math.pi / L * (np.outer(np.arange(F), shifts) % L)
    factor = 1.0 / (F * WINDOWS)
    parts = np.stack([np.cos(angle) * factor, -np.sin(angle) * factor])
    parts = parts.reshape(2, 128, 2, LAGS).transpose(2, 0, 1, 3)
    return parts.reshape(2 * F, LAGS).astype(ml_dtypes.bfloat16)


def normalise(record, band):
    x = record.reshape(SUB * NW, L).T
    magnitude = jnp.abs(x)
    runs = []
    for j in range(4):
        rows = band[64 if j == 0 else 0 : 320 if j == 3 else 384, :]
        run = jnp.dot(rows, magnitude[256 * j : 256 * j + 256], preferred_element_type=jnp.float32)
        blocks = [run[64 * i : 64 * i + 64] for i in range(run.shape[0] // 64)]
        runs.append([None] * (j == 0) + blocks + [None] * (j == 3))
    edge = lax.broadcasted_iota(jnp.int32, (64, 1), 0).astype(jnp.float32)
    pieces = []
    for i in range(16):
        j, place = divmod(i, 4)
        sums = runs[j][place + 1]
        if place == 0 and j > 0:
            sums = sums + runs[j - 1][5]
        if place == 3 and j < 3:
            sums = sums + runs[j + 1][0]
        inverse = 1.0 / (HALF + 1 + edge) if i == 0 else 1.0 / (2 * HALF - edge) if i == 15 else 1.0 / (2 * HALF + 1)
        pieces.append(x[64 * i : 64 * i + 64].astype(jnp.float32) / (sums * inverse + 1e-05))
    even = [(pieces[i] + pieces[i + 8]).astype(jnp.bfloat16) for i in range(8)]
    odd = [(pieces[i] - pieces[i + 8]).astype(jnp.bfloat16) for i in range(8)]
    return jnp.concatenate(even, axis=0), jnp.concatenate(odd, axis=0)


def transform(table, halves):
    return [jnp.dot(table[p], halves[p], preferred_element_type=jnp.float32) for p in range(2)]


def store_white(wide, spectra, flag, channel, out_ref):
    lanes = lax.broadcasted_iota(jnp.int32, (8, NW), 0)
    place = [8 * (v // 2) for v in range(32)]
    real = [spectra[v % 2][place[v] : place[v] + 8] for v in range(32)]
    imag = [spectra[v % 2][F // 2 + place[v] : F // 2 + place[v] + 8] for v in range(32)]
    power = [r * r + i * i for r, i in zip(real, imag)]
    before = [jnp.where(lanes == 0, 0.0, pltpu.roll(power[v], 1, 0)) for v in (30, 31)]
    after = [jnp.where(lanes == 7, 0.0, pltpu.roll(power[v], 7, 0)) for v in (0, 1)]
    padded = before + power + after
    total = power[0]
    for v in range(1, 32):
        total = total + power[v]
    floor = jnp.sum(total, axis=0, keepdims=True) * (0.1 / F) + 1e-06
    for v in range(32):
        smooth = padded[v] + padded[v + 1] + padded[v + 2] + padded[v + 3] + padded[v + 4]
        scale = lax.rsqrt(smooth * 0.2 + floor) * flag
        for s, part in ((0, real), (1, imag)):
            wide[pl.ds((2 * v + s) * 8 * PITCH + channel, 8, stride=PITCH), :] = part[v] * scale
            if channel == NC - 1:
                for u in range(8):
                    place = ((2 * v + s) * 8 + u) * PITCH
                    row = ((16 * u + v // 2) * 4 + 2 * s + v % 2) * NC
                    out_ref[row : row + NC, :] = wide[place : place + NC, :].astype(jnp.bfloat16)


def whiten_kernel(flags_hbm, record_hbm, table_hbm, out_ref, record, band, table, wide, flags, sems):
    count = NC // SUB
    parts = [pl.ds(t * SUB, SUB) for t in range(count)]
    copies = [pltpu.make_async_copy(record_hbm.at[p], record.at[p], sems.at[t]) for t, p in enumerate(parts)]
    copies += [
        pltpu.make_async_copy(table_hbm, table, sems.at[count]),
        pltpu.make_async_copy(flags_hbm, flags, sems.at[count + 1]),
    ]
    for t in [0, 1, count, count + 1, *range(2, count)]:
        copies[t].start()
    gap = lax.broadcasted_iota(jnp.int32, (384, 256), 0) - lax.broadcasted_iota(jnp.int32, (384, 256), 1) - 64
    band[...] = jnp.where(jnp.abs(gap) <= HALF, 1.0, 0.0).astype(jnp.bfloat16)
    halves, spectra = {}, {}
    for t in range(count + 2):
        if t < count:
            if t == 0:
                for copy in copies[:2]:
                    copy.wait()
            if t == 2:
                for copy in copies[2:count] + copies[count + 1 :]:
                    copy.wait()
            halves[t] = normalise(record[t * SUB : (t + 1) * SUB], band)
        if t == 1:
            copies[count].wait()
        if 0 <= t - 1 < count:
            spectra[t - 1] = transform(table, halves.pop(t - 1))
        if 0 <= t - 2 < count:
            even, odd = spectra.pop(t - 2)
            for c in range(SUB):
                cut = slice(c * NW, (c + 1) * NW)
                channel = (t - 2) * SUB + c
                store_white(wide, (even[:, cut], odd[:, cut]), flags[channel].astype(jnp.float32), channel, out_ref)


def whiten(record, flags):
    rows = 2 * F * NC
    white = pl.pallas_call(
        whiten_kernel,
        in_specs=[pl.BlockSpec(memory_space=pltpu.HBM)] * 3,
        out_specs=pl.BlockSpec(memory_space=pltpu.VMEM),
        out_shape=jax.ShapeDtypeStruct((rows, NW), jnp.bfloat16),
        scratch_shapes=[
            pltpu.VMEM((NC, NW, L), jnp.bfloat16),
            pltpu.VMEM((384, 256), jnp.bfloat16),
            pltpu.VMEM((2, F, L // 2), jnp.bfloat16),
            pltpu.VMEM((2 * F * PITCH, NW), jnp.float32),
            pltpu.SMEM((NC,), jnp.int32),
            pltpu.SemaphoreType.DMA((NC // SUB + 2,)),
        ],
        compiler_params=pltpu.CompilerParams(vmem_limit_bytes=40 * MIB),
        cost_estimate=pl.CostEstimate(flops=2 * 2048 * 1024 * 1024, bytes_accessed=8 * MIB, transcendentals=1 << 21),
    )(*[pltpu.with_memory_space_constraint(jnp.asarray(a), pltpu.HBM) for a in (flags, record, dft_rows())])
    return white.reshape(N_DEV, 4, NC, NW)


def cross_kernel(white_ref, out_ref):
    spectra = []
    for g in range(2):
        parts = []
        for s in range(2):
            for j in range(N_TM):
                parts.append(white_ref[:, j, 2 * s + g].reshape(CHANNELS, NW))
        local = jnp.concatenate(parts, axis=1)
        turned = jnp.concatenate([-p for p in parts[N_TM:]] + parts[:N_TM], axis=1)
        remote = []
        for j in range(N_TM):
            cut = slice(ND * j, ND * j + ND)
            remote += [local[cut], turned[cut]]
        spectra.append(
            lax.dot_general(
                local, jnp.concatenate(remote, axis=0), (((1,), (1,)), ((), ())), preferred_element_type=jnp.float32
            )
        )
    for j in range(N_TM):
        cut = slice(2 * ND * j, 2 * ND * (j + 1))
        block = jnp.concatenate([spectra[0][:, cut], spectra[1][:, cut]], axis=1)
        out_ref[:, j] = block.astype(jnp.bfloat16).reshape(N_CHAN, NC, 4 * ND)


def cross(white):
    out = pl.pallas_call(
        cross_kernel,
        out_shape=jax.ShapeDtypeStruct((N_CHAN, N_TM, NC, 4 * ND), jnp.bfloat16),
        compiler_params=pltpu.CompilerParams(vmem_limit_bytes=40 * MIB),
        cost_estimate=pl.CostEstimate(flops=1 << 30, bytes_accessed=3 * MIB, transcendentals=0),
    )(white.reshape(N_CHAN, N_TM, 4, NC, NW))
    return out.reshape(N_DEV, NC, 4 * ND)


def lags_kernel(cross_ref, table_ref, out_hbm, wide, lags, sems):
    for k in range(N_DEV):
        wide[k * PITCH : k * PITCH + NC, :] = cross_ref[k].astype(jnp.float32)
    copies = []
    for n in range(N_OUT):
        rows = []
        for c in range(n * NC // N_OUT, (n + 1) * NC // N_OUT):
            bins = wide[pl.ds(c, N_DEV, stride=PITCH), :].T.astype(jnp.bfloat16)
            rows.append(jnp.concatenate([bins[ND * q : ND * q + ND] for q in range(4)], axis=1))
        out = jnp.dot(jnp.concatenate(rows, axis=0), table_ref[...], preferred_element_type=jnp.float32)
        part = pl.ds(n * NC // N_OUT, NC // N_OUT)
        lags[part] = out.reshape(NC // N_OUT, ND, LAGS)
        copies.append(pltpu.make_async_copy(lags.at[part], out_hbm.at[part], sems.at[n]))
        copies[n].start()
    for copy in copies:
        copy.wait()


def to_lags(spectra):
    return pl.pallas_call(
        lags_kernel,
        out_shape=jax.ShapeDtypeStruct((NC, ND, LAGS), jnp.float32),
        out_specs=pl.BlockSpec(memory_space=pltpu.HBM),
        scratch_shapes=[
            pltpu.VMEM((N_DEV * PITCH, 4 * ND), jnp.float32),
            pltpu.VMEM((NC, ND, LAGS), jnp.float32),
            pltpu.SemaphoreType.DMA((N_OUT,)),
        ],
        compiler_params=pltpu.CompilerParams(vmem_limit_bytes=40 * MIB),
        cost_estimate=pl.CostEstimate(flops=1 << 28, bytes_accessed=2 * MIB, transcendentals=0),
    )(spectra, lag_rows())


def per_device(record, flags):
    white = lax.all_to_all(whiten(record, flags), BOTH, 0, 0, tiled=True)
    spectra = lax.all_to_all(cross(white), BOTH, 0, 0, tiled=True)
    return to_lags(spectra)


def solution(mesh):
    return jax.shard_map(
        per_device,
        mesh=mesh,
        in_specs=(P("chan", "tm", None), P("chan")),
        out_specs=P("chan", "tm", None),
        check_vma=False,
    )
```

```python
import math

import jax
import jax.numpy as jnp
import ml_dtypes
import numpy as np
from jax import lax
from jax.experimental import pallas as pl
from jax.experimental.pallas import tpu as pltpu
from jax.sharding import PartitionSpec as P

L = 1024
F = 256
LAGS = 512
HALF = 64
CHANNELS = 256
WINDOWS = 1024
BOTH = ("chan", "tm")

SUB = 2
PITCH = 17
NC = 16
NW = 128
ND = 32
N_CHAN = 16
N_TM = 8
N_DEV = 128
N_OUT = 4
MIB = 1 << 20


def dft_rows():
    phase = np.outer(np.arange(F), np.arange(L // 2)) % L
    angle = 2.0 * math.pi / L * phase
    parts = np.stack([np.cos(angle), -np.sin(angle)])
    parts = parts.reshape(2, 8, 16, 2, L // 2).transpose(3, 0, 2, 1, 4)
    return parts.reshape(2, F, L // 2).astype(ml_dtypes.bfloat16)


def lag_rows():
    shifts = np.arange(LAGS) - LAGS // 2
    angle = 2.0 * math.pi / L * (np.outer(np.arange(F), shifts) % L)
    factor = 1.0 / (F * WINDOWS)
    parts = np.stack([np.cos(angle) * factor, -np.sin(angle) * factor])
    parts = parts.reshape(2, 128, 2, LAGS).transpose(2, 0, 1, 3)
    return parts.reshape(2 * F, LAGS).astype(ml_dtypes.bfloat16)


def normalise(record, band):
    x = record.reshape(SUB * NW, L).T
    magnitude = jnp.abs(x)
    runs = []
    for j in range(4):
        rows = band[64 if j == 0 else 0 : 320 if j == 3 else 384, :]
        run = jnp.dot(rows, magnitude[256 * j : 256 * j + 256], preferred_element_type=jnp.float32)
        blocks = [run[64 * i : 64 * i + 64] for i in range(run.shape[0] // 64)]
        runs.append([None] * (j == 0) + blocks + [None] * (j == 3))
    edge = lax.broadcasted_iota(jnp.int32, (64, 1), 0).astype(jnp.float32)
    pieces = []
    for i in range(16):
        j, place = divmod(i, 4)
        sums = runs[j][place + 1]
        if place == 0 and j > 0:
            sums = sums + runs[j - 1][5]
        if place == 3 and j < 3:
            sums = sums + runs[j + 1][0]
        inverse = 1.0 / (HALF + 1 + edge) if i == 0 else 1.0 / (2 * HALF - edge) if i == 15 else 1.0 / (2 * HALF + 1)
        pieces.append(x[64 * i : 64 * i + 64].astype(jnp.float32) / (sums * inverse + 1e-05))
    even = [(pieces[i] + pieces[i + 8]).astype(jnp.bfloat16) for i in range(8)]
    odd = [(pieces[i] - pieces[i + 8]).astype(jnp.bfloat16) for i in range(8)]
    return jnp.concatenate(even, axis=0), jnp.concatenate(odd, axis=0)


def transform(table, halves):
    return [jnp.dot(table[p], halves[p], preferred_element_type=jnp.float32) for p in range(2)]


def store_white(wide, spectra, flag, channel, out_ref):
    lanes = lax.broadcasted_iota(jnp.int32, (8, NW), 0)
    place = [8 * (v // 2) for v in range(32)]
    real = [spectra[v % 2][place[v] : place[v] + 8] for v in range(32)]
    imag = [spectra[v % 2][F // 2 + place[v] : F // 2 + place[v] + 8] for v in range(32)]
    power = [r * r + i * i for r, i in zip(real, imag)]
    before = [jnp.where(lanes == 0, 0.0, pltpu.roll(power[v], 1, 0)) for v in (30, 31)]
    after = [jnp.where(lanes == 7, 0.0, pltpu.roll(power[v], 7, 0)) for v in (0, 1)]
    padded = before + power + after
    pairs = [padded[v] + padded[v + 1] for v in range(35)]
    total = power[0]
    for v in range(1, 32):
        total = total + power[v]
    floor = jnp.sum(total, axis=0, keepdims=True) * (0.1 / F) + 1e-06
    for v in range(32):
        smooth = pairs[v] + pairs[v + 2] + padded[v + 4]
        scale = lax.rsqrt(smooth * 0.2 + floor) * flag
        for s, part in ((0, real), (1, imag)):
            wide[pl.ds((2 * v + s) * 8 * PITCH + channel, 8, stride=PITCH), :] = part[v] * scale
            if channel == NC - 1:
                for u in range(8):
                    place = ((2 * v + s) * 8 + u) * PITCH
                    row = ((16 * u + v // 2) * 4 + 2 * s + v % 2) * NC
                    out_ref[row : row + NC, :] = wide[place : place + NC, :].astype(jnp.bfloat16)


def whiten_kernel(flags_hbm, record_hbm, table_hbm, out_ref, record, band, table, wide, flags, sems):
    count = NC // SUB
    parts = [pl.ds(t * SUB, SUB) for t in range(count)]
    copies = [pltpu.make_async_copy(record_hbm.at[p], record.at[p], sems.at[t]) for t, p in enumerate(parts)]
    copies += [
        pltpu.make_async_copy(table_hbm, table, sems.at[count]),
        pltpu.make_async_copy(flags_hbm, flags, sems.at[count + 1]),
    ]
    for t in [0, 1, count, count + 1, *range(2, count)]:
        copies[t].start()
    gap = lax.broadcasted_iota(jnp.int32, (384, 256), 0) - lax.broadcasted_iota(jnp.int32, (384, 256), 1) - 64
    band[...] = jnp.where(jnp.abs(gap) <= HALF, 1.0, 0.0).astype(jnp.bfloat16)
    halves, spectra = {}, {}
    for t in range(count + 2):
        if t < count:
            if t == 0:
                for copy in copies[:2]:
                    copy.wait()
            if t == 2:
                for copy in copies[2:count] + copies[count + 1 :]:
                    copy.wait()
            halves[t] = normalise(record[t * SUB : (t + 1) * SUB], band)
        if t == 1:
            copies[count].wait()
        if 0 <= t - 1 < count:
            spectra[t - 1] = transform(table, halves.pop(t - 1))
        if 0 <= t - 2 < count:
            even, odd = spectra.pop(t - 2)
            for c in range(SUB):
                cut = slice(c * NW, (c + 1) * NW)
                channel = (t - 2) * SUB + c
                store_white(wide, (even[:, cut], odd[:, cut]), flags[channel].astype(jnp.float32), channel, out_ref)


def whiten(record, flags):
    rows = 2 * F * NC
    white = pl.pallas_call(
        whiten_kernel,
        in_specs=[pl.BlockSpec(memory_space=pltpu.HBM)] * 3,
        out_specs=pl.BlockSpec(memory_space=pltpu.VMEM),
        out_shape=jax.ShapeDtypeStruct((rows, NW), jnp.bfloat16),
        scratch_shapes=[
            pltpu.VMEM((NC, NW, L), jnp.bfloat16),
            pltpu.VMEM((384, 256), jnp.bfloat16),
            pltpu.VMEM((2, F, L // 2), jnp.bfloat16),
            pltpu.VMEM(((2 * F + 8) * PITCH, NW), jnp.float32),
            pltpu.SMEM((NC,), jnp.int32),
            pltpu.SemaphoreType.DMA((NC // SUB + 2,)),
        ],
        compiler_params=pltpu.CompilerParams(vmem_limit_bytes=40 * MIB),
        cost_estimate=pl.CostEstimate(flops=2 * 2048 * 1024 * 1024, bytes_accessed=8 * MIB, transcendentals=1 << 21),
    )(*[pltpu.with_memory_space_constraint(jnp.asarray(a), pltpu.HBM) for a in (flags, record, dft_rows())])
    return white.reshape(N_DEV, 4, NC, NW)


def cross_kernel(white_ref, out_ref):
    spectra = []
    for g in range(2):
        parts = []
        for s in range(2):
            for j in range(N_TM):
                parts.append(white_ref[:, j, 2 * s + g].reshape(CHANNELS, NW))
        local = jnp.concatenate(parts, axis=1)
        turned = jnp.concatenate([-p for p in parts[N_TM:]] + parts[:N_TM], axis=1)
        remote = []
        for j in range(N_TM):
            cut = slice(ND * j, ND * j + ND)
            remote += [local[cut], turned[cut]]
        spectra.append(
            lax.dot_general(
                local, jnp.concatenate(remote, axis=0), (((1,), (1,)), ((), ())), preferred_element_type=jnp.float32
            )
        )
    for j in range(N_TM):
        cut = slice(2 * ND * j, 2 * ND * (j + 1))
        block = jnp.concatenate([spectra[0][:, cut], spectra[1][:, cut]], axis=1)
        out_ref[:, j] = block.astype(jnp.bfloat16).reshape(N_CHAN, NC, 4 * ND)


def cross(white):
    out = pl.pallas_call(
        cross_kernel,
        out_shape=jax.ShapeDtypeStruct((N_CHAN, N_TM, NC, 4 * ND), jnp.bfloat16),
        compiler_params=pltpu.CompilerParams(vmem_limit_bytes=40 * MIB),
        cost_estimate=pl.CostEstimate(flops=1 << 30, bytes_accessed=3 * MIB, transcendentals=0),
    )(white.reshape(N_CHAN, N_TM, 4, NC, NW))
    return out.reshape(N_DEV, NC, 4 * ND)


def lags_kernel(cross_ref, table_ref, out_hbm, wide, lags, sems):
    for k in range(N_DEV):
        wide[k * PITCH : k * PITCH + NC, :] = cross_ref[k].astype(jnp.float32)
    copies = []
    for n in range(N_OUT):
        rows = []
        for c in range(n * NC // N_OUT, (n + 1) * NC // N_OUT):
            bins = wide[pl.ds(c, N_DEV, stride=PITCH), :].T.astype(jnp.bfloat16)
            rows.append(jnp.concatenate([bins[ND * q : ND * q + ND] for q in range(4)], axis=1))
        out = jnp.dot(jnp.concatenate(rows, axis=0), table_ref[...], preferred_element_type=jnp.float32)
        part = pl.ds(n * NC // N_OUT, NC // N_OUT)
        lags[part] = out.reshape(NC // N_OUT, ND, LAGS)
        copies.append(pltpu.make_async_copy(lags.at[part], out_hbm.at[part], sems.at[n]))
        copies[n].start()
    for copy in copies:
        copy.wait()


def to_lags(spectra):
    return pl.pallas_call(
        lags_kernel,
        out_shape=jax.ShapeDtypeStruct((NC, ND, LAGS), jnp.float32),
        out_specs=pl.BlockSpec(memory_space=pltpu.HBM),
        scratch_shapes=[
            pltpu.VMEM(((N_DEV + 8) * PITCH, 4 * ND), jnp.float32),
            pltpu.VMEM((NC, ND, LAGS), jnp.float32),
            pltpu.SemaphoreType.DMA((N_OUT,)),
        ],
        compiler_params=pltpu.CompilerParams(vmem_limit_bytes=40 * MIB),
        cost_estimate=pl.CostEstimate(flops=1 << 28, bytes_accessed=2 * MIB, transcendentals=0),
    )(spectra, lag_rows())


def per_device(record, flags):
    white = lax.all_to_all(whiten(record, flags), BOTH, 0, 0, tiled=True)
    spectra = lax.all_to_all(cross(white), BOTH, 0, 0, tiled=True)
    return to_lags(spectra)


def solution(mesh):
    return jax.shard_map(
        per_device,
        mesh=mesh,
        in_specs=(P("chan", "tm", None), P("chan")),
        out_specs=P("chan", "tm", None),
        check_vma=False,
    )
```

```python
import math

import jax
import jax.numpy as jnp
import ml_dtypes
import numpy as np
from jax import lax
from jax.experimental import pallas as pl
from jax.experimental.pallas import tpu as pltpu
from jax.sharding import PartitionSpec as P

L = 1024
F = 256
LAGS = 512
HALF = 64
CHANNELS = 256
WINDOWS = 1024
BOTH = ("chan", "tm")

SUB = 2
PITCH = 17
NC = 16
NW = 128
ND = 32
N_CHAN = 16
N_TM = 8
N_DEV = 128
N_OUT = 4
MIB = 1 << 20


def dft_rows():
    phase = np.outer(np.arange(F), np.arange(L // 2)) % L
    angle = 2.0 * math.pi / L * phase
    parts = np.stack([np.cos(angle), -np.sin(angle)])
    parts = parts.reshape(2, 8, 16, 2, L // 2).transpose(3, 0, 2, 1, 4)
    return parts.reshape(2, F, L // 2).astype(ml_dtypes.bfloat16)


def lag_rows():
    shifts = np.arange(LAGS) - LAGS // 2
    angle = 2.0 * math.pi / L * (np.outer(np.arange(F), shifts) % L)
    factor = 1.0 / (F * WINDOWS)
    parts = np.stack([np.cos(angle) * factor, -np.sin(angle) * factor])
    parts = parts.reshape(2, 128, 2, LAGS).transpose(2, 0, 1, 3)
    return parts.reshape(2 * F, LAGS).astype(ml_dtypes.bfloat16)


def normalise(record, band):
    x = record.reshape(SUB * NW, L).T
    magnitude = jnp.abs(x)
    runs = []
    for j in range(4):
        rows = band[64 if j == 0 else 0 : 320 if j == 3 else 384, :]
        run = jnp.dot(rows, magnitude[256 * j : 256 * j + 256], preferred_element_type=jnp.float32)
        blocks = [run[64 * i : 64 * i + 64] for i in range(run.shape[0] // 64)]
        runs.append([None] * (j == 0) + blocks + [None] * (j == 3))
    edge = lax.broadcasted_iota(jnp.int32, (64, 1), 0).astype(jnp.float32)
    pieces = []
    for i in range(16):
        j, place = divmod(i, 4)
        sums = runs[j][place + 1]
        if place == 0 and j > 0:
            sums = sums + runs[j - 1][5]
        if place == 3 and j < 3:
            sums = sums + runs[j + 1][0]
        inverse = 1.0 / (HALF + 1 + edge) if i == 0 else 1.0 / (2 * HALF - edge) if i == 15 else 1.0 / (2 * HALF + 1)
        pieces.append(x[64 * i : 64 * i + 64] * (1.0 / (sums * inverse + 1e-05)).astype(jnp.bfloat16))
    even = [pieces[i] + pieces[i + 8] for i in range(8)]
    odd = [pieces[i] - pieces[i + 8] for i in range(8)]
    return jnp.concatenate(even, axis=0), jnp.concatenate(odd, axis=0)


def transform(table, halves):
    return [jnp.dot(table[p], halves[p], preferred_element_type=jnp.float32) for p in range(2)]


def store_white(wide, spectra, flag, channel, out_ref):
    lanes = lax.broadcasted_iota(jnp.int32, (8, NW), 0)
    place = [8 * (v // 2) for v in range(32)]
    real = [spectra[v % 2][place[v] : place[v] + 8] for v in range(32)]
    imag = [spectra[v % 2][F // 2 + place[v] : F // 2 + place[v] + 8] for v in range(32)]
    power = [r * r + i * i for r, i in zip(real, imag)]
    before = [jnp.where(lanes == 0, 0.0, pltpu.roll(power[v], 1, 0)) for v in (30, 31)]
    after = [jnp.where(lanes == 7, 0.0, pltpu.roll(power[v], 7, 0)) for v in (0, 1)]
    padded = before + power + after
    pairs = [padded[v] + padded[v + 1] for v in range(35)]
    total = power[0]
    for v in range(1, 32):
        total = total + power[v]
    floor = jnp.sum(total, axis=0, keepdims=True) * (0.1 / F) + 1e-06
    for v in range(32):
        smooth = pairs[v] + pairs[v + 2] + padded[v + 4]
        scale = lax.rsqrt(smooth * 0.2 + floor) * flag
        for s, part in ((0, real), (1, imag)):
            wide[pl.ds((2 * v + s) * 8 * PITCH + channel, 8, stride=PITCH), :] = part[v] * scale
            if channel == NC - 1:
                for u in range(8):
                    place = ((2 * v + s) * 8 + u) * PITCH
                    row = ((16 * u + v // 2) * 4 + 2 * s + v % 2) * NC
                    out_ref[row : row + NC, :] = wide[place : place + NC, :].astype(jnp.bfloat16)


def whiten_kernel(flags_hbm, record_hbm, table_hbm, out_ref, record, band, table, wide, flags, sems):
    count = NC // SUB
    parts = [pl.ds(t * SUB, SUB) for t in range(count)]
    copies = [pltpu.make_async_copy(record_hbm.at[p], record.at[p], sems.at[t]) for t, p in enumerate(parts)]
    copies += [
        pltpu.make_async_copy(table_hbm, table, sems.at[count]),
        pltpu.make_async_copy(flags_hbm, flags, sems.at[count + 1]),
    ]
    for t in [0, 1, count, count + 1, *range(2, count)]:
        copies[t].start()
    gap = lax.broadcasted_iota(jnp.int32, (384, 256), 0) - lax.broadcasted_iota(jnp.int32, (384, 256), 1) - 64
    band[...] = jnp.where(jnp.abs(gap) <= HALF, 1.0, 0.0).astype(jnp.bfloat16)
    halves, spectra = {}, {}
    for t in range(count + 2):
        if t < count:
            if t == 0:
                for copy in copies[:2]:
                    copy.wait()
            if t == 2:
                for copy in copies[2:count] + copies[count + 1 :]:
                    copy.wait()
            halves[t] = normalise(record[t * SUB : (t + 1) * SUB], band)
        if t == 1:
            copies[count].wait()
        if 0 <= t - 1 < count:
            spectra[t - 1] = transform(table, halves.pop(t - 1))
        if 0 <= t - 2 < count:
            even, odd = spectra.pop(t - 2)
            for c in range(SUB):
                cut = slice(c * NW, (c + 1) * NW)
                channel = (t - 2) * SUB + c
                store_white(wide, (even[:, cut], odd[:, cut]), flags[channel].astype(jnp.float32), channel, out_ref)


def whiten(record, flags):
    rows = 2 * F * NC
    white = pl.pallas_call(
        whiten_kernel,
        in_specs=[pl.BlockSpec(memory_space=pltpu.HBM)] * 3,
        out_specs=pl.BlockSpec(memory_space=pltpu.VMEM),
        out_shape=jax.ShapeDtypeStruct((rows, NW), jnp.bfloat16),
        scratch_shapes=[
            pltpu.VMEM((NC, NW, L), jnp.bfloat16),
            pltpu.VMEM((384, 256), jnp.bfloat16),
            pltpu.VMEM((2, F, L // 2), jnp.bfloat16),
            pltpu.VMEM(((2 * F + 8) * PITCH, NW), jnp.float32),
            pltpu.SMEM((NC,), jnp.int32),
            pltpu.SemaphoreType.DMA((NC // SUB + 2,)),
        ],
        compiler_params=pltpu.CompilerParams(vmem_limit_bytes=40 * MIB),
        cost_estimate=pl.CostEstimate(flops=2 * 2048 * 1024 * 1024, bytes_accessed=8 * MIB, transcendentals=1 << 21),
    )(*[pltpu.with_memory_space_constraint(jnp.asarray(a), pltpu.HBM) for a in (flags, record, dft_rows())])
    return white.reshape(N_DEV, 4, NC, NW)


def cross_kernel(white_ref, out_ref):
    spectra = []
    for g in range(2):
        parts = []
        for s in range(2):
            for j in range(N_TM):
                parts.append(white_ref[:, j, 2 * s + g].reshape(CHANNELS, NW))
        local = jnp.concatenate(parts, axis=1)
        turned = jnp.concatenate([-p for p in parts[N_TM:]] + parts[:N_TM], axis=1)
        remote = []
        for j in range(N_TM):
            cut = slice(ND * j, ND * j + ND)
            remote += [local[cut], turned[cut]]
        spectra.append(
            lax.dot_general(
                local, jnp.concatenate(remote, axis=0), (((1,), (1,)), ((), ())), preferred_element_type=jnp.float32
            )
        )
    for j in range(N_TM):
        cut = slice(2 * ND * j, 2 * ND * (j + 1))
        block = jnp.concatenate([spectra[0][:, cut], spectra[1][:, cut]], axis=1)
        out_ref[:, j] = block.astype(jnp.bfloat16).reshape(N_CHAN, NC, 4 * ND)


def cross(white):
    out = pl.pallas_call(
        cross_kernel,
        out_shape=jax.ShapeDtypeStruct((N_CHAN, N_TM, NC, 4 * ND), jnp.bfloat16),
        compiler_params=pltpu.CompilerParams(vmem_limit_bytes=40 * MIB),
        cost_estimate=pl.CostEstimate(flops=1 << 30, bytes_accessed=3 * MIB, transcendentals=0),
    )(white.reshape(N_CHAN, N_TM, 4, NC, NW))
    return out.reshape(N_DEV, NC, 4 * ND)


def lags_kernel(cross_ref, table_ref, out_hbm, wide, lags, sems):
    for k in range(N_DEV):
        wide[k * PITCH : k * PITCH + NC, :] = cross_ref[k].astype(jnp.float32)
    copies = []
    for n in range(N_OUT):
        rows = []
        for c in range(n * NC // N_OUT, (n + 1) * NC // N_OUT):
            bins = wide[pl.ds(c, N_DEV, stride=PITCH), :].T.astype(jnp.bfloat16)
            rows.append(jnp.concatenate([bins[ND * q : ND * q + ND] for q in range(4)], axis=1))
        out = jnp.dot(jnp.concatenate(rows, axis=0), table_ref[...], preferred_element_type=jnp.float32)
        part = pl.ds(n * NC // N_OUT, NC // N_OUT)
        lags[part] = out.reshape(NC // N_OUT, ND, LAGS)
        copies.append(pltpu.make_async_copy(lags.at[part], out_hbm.at[part], sems.at[n]))
        copies[n].start()
    for copy in copies:
        copy.wait()


def to_lags(spectra):
    return pl.pallas_call(
        lags_kernel,
        out_shape=jax.ShapeDtypeStruct((NC, ND, LAGS), jnp.float32),
        out_specs=pl.BlockSpec(memory_space=pltpu.HBM),
        scratch_shapes=[
            pltpu.VMEM(((N_DEV + 8) * PITCH, 4 * ND), jnp.float32),
            pltpu.VMEM((NC, ND, LAGS), jnp.float32),
            pltpu.SemaphoreType.DMA((N_OUT,)),
        ],
        compiler_params=pltpu.CompilerParams(vmem_limit_bytes=40 * MIB),
        cost_estimate=pl.CostEstimate(flops=1 << 28, bytes_accessed=2 * MIB, transcendentals=0),
    )(spectra, lag_rows())


def per_device(record, flags):
    white = lax.all_to_all(whiten(record, flags), BOTH, 0, 0, tiled=True)
    spectra = lax.all_to_all(cross(white), BOTH, 0, 0, tiled=True)
    return to_lags(spectra)


def solution(mesh):
    return jax.shard_map(
        per_device,
        mesh=mesh,
        in_specs=(P("chan", "tm", None), P("chan")),
        out_specs=P("chan", "tm", None),
        check_vma=False,
    )
```
